256 devices in a mesh: subj: 32 (over y, z), var: 8 (over x, core).
Axes of the slice: x: 4, y: 4, z: 8, core: 2. Of those that a mesh axis runs over, the one named last changes fastest.
Arguments:
- genotype: bfloat16 [32768, 32768], P('subj', 'var'), may hold values from -6 to 6
- coefs: bfloat16 [32768, 48], P('var'), may hold values from -0.03125 to 0.03125
- events: int32 [32768], P('subj'), may hold values 0 or 1
- folds: int32 [32768, 48], P('subj'), may hold values 0 or 1
- groups: int32 [32768], P('subj'), may hold values from 0 to 2015, as said below
Outputs:
- gradient: float32 [32768, 48], P(('var', 'subj'))
The draws below stay inside these ranges and needn't reach their ends.
Inputs may be any that keep to these rules, and one draw needn't show every extreme that they name: groups never fall along the subjects; every group holds 1 to 32 consecutive subjects; each aligned block of 1024 subjects holds whole groups only, 63 of them, one exactly 32; every group number occurs.
All inputs are finite; a program needn't handle non-finite values. No bound on the sum of `events` or of `folds` on one device may be relied on, other than what follows from the above.
Results may differ from the reference program's by a relative error of at most 0.0026.
Values may be sent and summed in bfloat16 or wider, within the bound.
No kernel may reach another device: no remote copies, remote signals or barrier semaphores. Data moves between devices by JAX's collectives and lax.ppermute only.
A program may use at most 64 MiB of HBM per device.

```python
import jax
import jax.numpy as jnp
from jax import lax

VARIANTS = 32768
COLS = 48
ROWS = 1024
MAXTIE = 32
SUBJECTS = 32768
TIEGROUPS = 2016


def draw_groups(key, part):
    key = jax.random.fold_in(key, 7)
    blocks = SUBJECTS // ROWS
    pairs = ROWS // MAXTIE
    cut_key, whole_key = jax.random.split(key)
    cuts = jax.random.randint(cut_key, (blocks, pairs, 1), 1, MAXTIE, dtype=jnp.int32)
    whole = jax.random.randint(whole_key, (blocks, 1, 1), 0, pairs, dtype=jnp.int32)
    slot = jnp.arange(MAXTIE, dtype=jnp.int32)[None, None, :]
    pair = jnp.arange(pairs, dtype=jnp.int32)[None, :, None]
    later = (slot >= cuts).astype(jnp.int32) * (pair != whole).astype(jnp.int32)
    local = 2 * pair + later - (pair > whole).astype(jnp.int32)
    base = jnp.arange(blocks, dtype=jnp.int32)[:, None, None] * (2 * pairs - 1)
    return (base + local).reshape(SUBJECTS).astype(jnp.int32)


def place_ends(entries, key, least, high):
    shape = entries.shape
    spot = [jax.random.randint(jax.random.fold_in(key, axis), (), 0, shape[axis]) for axis in range(len(shape))]
    entries = entries.at[tuple(spot)].set(least)
    longest = shape.index(max(shape))
    spot[longest] = (spot[longest] + 1) % shape[longest]
    return entries.at[tuple(spot)].set(high)


def steps_of(own_key, extent, pieces, low, largest):
    def one(dim, blocks):
        draws = jax.random.uniform(jax.random.fold_in(jax.random.fold_in(own_key, 6), dim), (blocks,), jnp.float32, low / len(pieces), largest / len(pieces))
        return jnp.repeat(jnp.exp(draws), extent[dim] // blocks).reshape((-1,) + (1,) * (len(extent) - dim - 1))

    gain = one(*pieces[0])
    for cut in pieces[1:]:
        gain = gain * one(*cut)
    return gain


def centred(own_key, shape, scale, bound, cuts=(), held_as=jnp.bfloat16):
    values = scale * jax.random.normal(own_key, shape, jnp.float32)
    if cuts:
        values = values * steps_of(own_key, shape, cuts, -0.22, 0.18)
    return jnp.clip(values, -bound, bound).astype(held_as)


def setup_inputs(seed: int = 0) -> dict:
    key_of = jax.random.split(jax.random.key(seed), 6)
    return {
        "genotype": centred(key_of[0], (SUBJECTS, VARIANTS), 1.0, 6.0, ((0, 32), (1, 8))),
        "coefs": centred(key_of[1], (VARIANTS, COLS), VARIANTS ** -0.5, 0.03125, ((0, 8),)),
        "events": place_ends((jax.random.randint(key_of[2], (SUBJECTS,), 0, 3) < 1).astype(jnp.int32), jax.random.fold_in(key_of[2], 1), 0, 1),
        "folds": place_ends((jax.random.randint(key_of[3], (SUBJECTS, COLS), 0, 5) < 4).astype(jnp.int32), jax.random.fold_in(key_of[3], 1), 0, 1),
        "groups": draw_groups(jax.random.fold_in(key_of[5], 71), 0),
    }


def reference(genotype, coefs, events, folds, groups):
    eta = jnp.dot(genotype, coefs, preferred_element_type=jnp.float32)
    risk_weight = folds.astype(jnp.float32) * jnp.exp(eta)
    counted = (events[:, None] * folds).astype(jnp.float32)
    position = jnp.arange(SUBJECTS, dtype=jnp.int32)
    starts = jax.ops.segment_min(position, groups, num_segments=TIEGROUPS)
    finish = jax.ops.segment_max(position, groups, num_segments=TIEGROUPS)
    suffix = jnp.cumsum(risk_weight[::-1], axis=0)[::-1]
    risk_sum = suffix[starts[groups]]
    inverse = counted / jnp.where(counted > 0, risk_sum, 1.0)
    hazard = jnp.cumsum(inverse, axis=0)[finish[groups]]
    resid = (counted - risk_weight * hazard).astype(jnp.bfloat16)
    total = lax.dot_general(genotype, resid, (((0,), (0,)), ((), ())), preferred_element_type=jnp.float32)
    return total * (-1.0 / jnp.sqrt(jnp.float32(SUBJECTS)))
```

```python
import functools

import jax
import jax.numpy as jnp
from jax import lax
from jax.experimental import pallas as pl
from jax.experimental.pallas import tpu as pltpu
from jax.sharding import PartitionSpec as P

COLS = 48
OWN = 6
ROWS = 1024
SLOTS = 64
VMEM = 40 * 1024 * 1024

SEND = jnp.bfloat16


def gray(value):
    return value ^ (value >> 1)


def var_label(index):
    return (index & 1) * 4 + gray(index >> 1)


def subj_label(index):
    y = gray(index >> 3)
    z = gray(index & 7)
    return (
        (y & 1) * 16 + (z & 1) * 8 + ((y >> 1) & 1) * 4 + ((z >> 1) & 1) * 2 + ((z >> 2) & 1)
    )


def exchange(value, axis, count, label, mask):
    labels = [label(index) for index in range(count)]
    where = {l: index for index, l in enumerate(labels)}
    pairs = [(index, where[labels[index] ^ mask]) for index in range(count)]
    return lax.ppermute(value, axis, pairs)


def parts3(value):
    high = value.astype(jnp.bfloat16)
    rest = value - high.astype(jnp.float32)
    mid = rest.astype(jnp.bfloat16)
    low = (rest - mid.astype(jnp.float32)).astype(jnp.bfloat16)
    return high, mid, low


def params():
    return pltpu.CompilerParams(vmem_limit_bytes=VMEM)


def one_hot(groups_ref, base):
    slot = lax.broadcasted_iota(jnp.int32, (SLOTS, ROWS), 0)
    return (slot == groups_ref[...] - base).astype(jnp.bfloat16)


def eta_kernel(where_ref, geno_ref, coefs_ref, out_ref):
    label = where_ref[0]
    step = pl.program_id(0)
    width = geno_ref.shape[0]
    block = jnp.dot(geno_ref[...], coefs_ref[...], preferred_element_type=jnp.float32)
    turned = block.T
    at = pl.ds(pl.multiple_of(step * width, 128), width)
    for chunk in range(8):
        out_ref[chunk ^ label, :, at] = turned[OWN * chunk : OWN * chunk + OWN, :]


def eta_slots(where, genotype, coefs):
    rows, depth = genotype.shape
    block = 256
    return pl.pallas_call(
        eta_kernel,
        grid_spec=pltpu.PrefetchScalarGridSpec(
            num_scalar_prefetch=1,
            grid=(rows // block,),
            in_specs=[
                pl.BlockSpec((block, depth), lambda i, w: (i, 0)),
                pl.BlockSpec((depth, COLS), lambda i, w: (0, 0)),
            ],
            out_specs=pl.BlockSpec((8, OWN, rows), lambda i, w: (0, 0, 0)),
        ),
        out_shape=jax.ShapeDtypeStruct((8, OWN, rows), jnp.float32),
        compiler_params=params(),
        cost_estimate=pl.CostEstimate(
            flops=2 * rows * depth * 128, bytes_accessed=rows * depth * 2, transcendentals=0
        ),
    )(where, genotype, coefs)


def count_kernel(where_ref, folds_ref, events_ref, groups_ref, fold_ref, counted_ref, count_ref):
    label = where_ref[0]
    base = where_ref[2]
    row = lax.broadcasted_iota(jnp.int32, (OWN, COLS), 0)
    col = lax.broadcasted_iota(jnp.int32, (OWN, COLS), 1)
    pick = (col == row + OWN * label).astype(jnp.bfloat16)
    fold = lax.dot_general(
        pick,
        folds_ref[...].astype(jnp.bfloat16),
        (((1,), (1,)), ((), ())),
        preferred_element_type=jnp.float32,
    )
    counted = fold * events_ref[...].astype(jnp.float32)
    hot = one_hot(groups_ref, base)
    fold_ref[...] = fold
    counted_ref[...] = counted
    count_ref[...] = lax.dot_general(
        counted.astype(jnp.bfloat16), hot, (((1,), (1,)), ((), ())), preferred_element_type=jnp.float32
    )


def smem():
    return pl.BlockSpec(memory_space=pltpu.SMEM)


def vmem():
    return pl.BlockSpec(memory_space=pltpu.VMEM)


def counts(where, folds, events, groups):
    return pl.pallas_call(
        count_kernel,
        in_specs=[smem(), vmem(), vmem(), vmem()],
        out_specs=[vmem()] * 3,
        out_shape=[
            jax.ShapeDtypeStruct((OWN, ROWS), jnp.float32),
            jax.ShapeDtypeStruct((OWN, ROWS), jnp.float32),
            jax.ShapeDtypeStruct((OWN, SLOTS), jnp.float32),
        ],
        compiler_params=params(),
        cost_estimate=pl.CostEstimate(flops=10**8, bytes_accessed=10**6, transcendentals=0),
    )(where, folds, events, groups)


def weight_kernel(where_ref, eta_ref, more_ref, fold_ref, count_ref, groups_ref, weight_ref, pack_ref):
    base = where_ref[2]
    eta = eta_ref[0] + more_ref[0]
    weight = fold_ref[...] * jnp.exp(eta)
    weight_ref[...] = weight
    hot = one_hot(groups_ref, base)
    total = jnp.zeros((OWN, SLOTS), jnp.float32)
    for part in parts3(weight):
        total += lax.dot_general(
            part, hot, (((1,), (1,)), ((), ())), preferred_element_type=jnp.float32
        )
    pack_ref[0, :, :SLOTS] = total
    pack_ref[0, :, SLOTS:] = count_ref[...]


def weights(where, eta, more, fold, count, groups):
    return pl.pallas_call(
        weight_kernel,
        in_specs=[smem()] + [vmem()] * 5,
        out_specs=[vmem()] * 2,
        out_shape=[
            jax.ShapeDtypeStruct((OWN, ROWS), jnp.float32),
            jax.ShapeDtypeStruct((1, OWN, 2 * SLOTS), jnp.float32),
        ],
        compiler_params=params(),
        cost_estimate=pl.CostEstimate(flops=10**8, bytes_accessed=10**6, transcendentals=0),
    )(where, eta, more, fold, count, groups)


def resid_kernel(where_ref, near_ref, far_ref, weight_ref, counted_ref, groups_ref, resid_ref):
    label = where_ref[1]
    base = where_ref[2]
    mine = where_ref[3]
    half = near_ref.shape[0]
    lane = lax.broadcasted_iota(jnp.int32, (OWN, 2 * SLOTS), 1)
    first = lane < SLOTS
    zero = jnp.zeros((OWN, 2 * SLOTS), jnp.float32)
    after = zero
    before = zero
    own = zero
    for device in reversed(range(2 * half)):
        slot = label ^ subj_label(device)
        low = slot & (half - 1)
        tile = jnp.where(slot < half, near_ref[low], far_ref[low])
        suffix = jnp.where(first, tile, 0.0)
        shift = 1
        while shift < SLOTS:
            suffix = suffix + pltpu.roll(suffix, 2 * SLOTS - shift, 1)
            shift *= 2
        total = suffix + pltpu.roll(suffix, SLOTS, 1)
        count = pltpu.roll(tile, SLOTS, 1)
        some = first & (count > 0)
        risk = jnp.where(some, suffix + after, 1.0)
        added = jnp.where(some, count / risk, 0.0)
        after = after + total
        before = before + jnp.where(device < mine, added, 0.0)
        own = own + jnp.where(device == mine, added, 0.0)
    shift = 1
    prefix = own
    while shift < SLOTS:
        prefix = prefix + pltpu.roll(prefix, shift, 1)
        before = before + pltpu.roll(before, shift, 1)
        shift *= 2
    before = before + pltpu.roll(before, SLOTS, 1)
    hazard = (prefix + before)[:, :SLOTS]
    hot = one_hot(groups_ref, base)
    spread = jnp.zeros((OWN, ROWS), jnp.float32)
    for part in parts3(hazard):
        spread += jnp.dot(part, hot, preferred_element_type=jnp.float32)
    resid = counted_ref[...] - weight_ref[...] * spread
    resid_ref[0] = resid.astype(jnp.bfloat16)


def residuals(where, near, far, weight, counted, groups):
    return pl.pallas_call(
        resid_kernel,
        in_specs=[smem()] + [vmem()] * 5,
        out_specs=vmem(),
        out_shape=jax.ShapeDtypeStruct((1, OWN, ROWS), jnp.bfloat16),
        compiler_params=params(),
        cost_estimate=pl.CostEstimate(flops=10**8, bytes_accessed=10**6, transcendentals=0),
    )(where, near, far, weight, counted, groups)


def grad_kernel(far, factor, where_ref, geno_ref, near_ref, other_ref, out_ref, turned):
    var = where_ref[0]
    label = where_ref[1]
    step = pl.program_id(0)

    @pl.when(step == 0)
    def _():
        for chunk in range(8):
            slot = chunk ^ var
            low = slot & 3
            piece = jnp.where(
                slot < 4, near_ref[low].astype(jnp.float32), other_ref[low].astype(jnp.float32)
            )
            turned[OWN * chunk : OWN * chunk + OWN, :] = piece

    block = jnp.dot(
        turned[...].astype(jnp.bfloat16), geno_ref[...], preferred_element_type=jnp.float32
    )
    block = (block * factor).astype(out_ref.dtype)
    count = geno_ref.shape[1] // 128
    start = block_index(far, step, label, count) * count
    for piece in range(count):
        slot = (subj_label(start + piece) ^ label) & 15
        out_ref[slot] = block[:, 128 * piece : 128 * piece + 128]


def block_index(far, step, label, count):
    per_y = 8 // count
    bit = (label >> 4) & 1
    wanted = bit ^ 1 if far else bit
    y_pick = step // per_y
    y = jnp.where(wanted == 1, 1 + y_pick, 3 * y_pick)
    return y * per_y + lax.rem(step, per_y)


def grad_slots(far, dtype, factor, where, genotype, near, other):
    rows, depth = genotype.shape
    block = 512
    count = block // 128
    return pl.pallas_call(
        functools.partial(grad_kernel, far, factor),
        grid_spec=pltpu.PrefetchScalarGridSpec(
            num_scalar_prefetch=1,
            grid=(depth // block // 2,),
            in_specs=[
                pl.BlockSpec((rows, block), lambda i, w: (0, block_index(far, i, w[1], count))),
                pl.BlockSpec((4, OWN, rows), lambda i, w: (0, 0, 0)),
                pl.BlockSpec((4, OWN, rows), lambda i, w: (0, 0, 0)),
            ],
            out_specs=pl.BlockSpec((16, COLS, 128), lambda i, w: (0, 0, 0)),
            scratch_shapes=[pltpu.VMEM((COLS, rows), jnp.float32)],
        ),
        out_shape=jax.ShapeDtypeStruct((16, COLS, 128), dtype),
        compiler_params=params(),
        cost_estimate=pl.CostEstimate(
            flops=rows * depth * 128, bytes_accessed=rows * depth, transcendentals=0
        ),
    )(where, genotype, near, other)


def per_device(genotype, coefs, events, folds, groups):
    subj = lax.axis_index("subj")
    var = lax.axis_index("var")
    across = functools.partial(exchange, axis="var", count=8, label=var_label)
    along = functools.partial(exchange, axis="subj", count=32, label=subj_label)
    where = jnp.stack(
        [var_label(var), subj_label(subj), subj * 63, subj]
    ).astype(jnp.int32)
    events = events.reshape(1, ROWS)
    groups = groups.reshape(1, ROWS)
    factor = -1.0 / float(32 * ROWS) ** 0.5

    eta = eta_slots(where, genotype, coefs)
    fold, counted, count = counts(where, folds, events, groups)
    eta = eta[:4] + across(eta[4:], mask=4)
    eta = eta[:2] + across(eta[2:], mask=2)
    more = across(eta[1:], mask=1)
    weight, pack = weights(where, eta, more, fold, count, groups)

    for mask in (1, 2, 4, 8):
        pack = jnp.concatenate([pack, along(pack, mask=mask)], axis=0)
    far = along(pack, mask=16)
    resid = residuals(where, pack, far, weight, counted, groups)

    for mask in (1, 2):
        resid = jnp.concatenate([resid, across(resid, mask=mask)], axis=0)
    other = across(resid, mask=4)

    sent = grad_slots(True, SEND, factor, where, genotype, resid, other)
    kept = grad_slots(False, jnp.float32, factor, where, genotype, resid, other)
    total = kept + along(sent, mask=16).astype(jnp.float32)
    for mask in (8, 4, 2, 1):
        out = total[mask:]
        if mask == 8:
            out = out.astype(SEND)
        total = total[:mask] + along(out, mask=mask).astype(jnp.float32)
    return total[0].T


def solution(mesh):
    in_specs = (P("subj", "var"), P("var", None), P("subj"), P("subj", None), P("subj"))
    out_specs = P(("var", "subj"), None)
    return jax.shard_map(
        per_device, mesh=mesh, in_specs=in_specs, out_specs=out_specs, check_vma=False
    )
```

```python
import functools

import jax
import jax.numpy as jnp
from jax import lax
from jax.experimental import pallas as pl
from jax.experimental.pallas import tpu as pltpu
from jax.sharding import PartitionSpec as P

COLS = 48
HALF = 24
ROWS = 1024
SLOTS = 64
COUNT = 32
MIB = 1024 * 1024
SCALE = 0.125


def parts3(value):
    high = value.astype(jnp.bfloat16)
    rest = value - high.astype(jnp.float32)
    mid = rest.astype(jnp.bfloat16)
    low = (rest - mid.astype(jnp.float32)).astype(jnp.bfloat16)
    return high, mid, low


def smem():
    return pl.BlockSpec(memory_space=pltpu.SMEM)


def vmem():
    return pl.BlockSpec(memory_space=pltpu.VMEM)


def eta_kernel(where_ref, geno_ref, coefs_ref, out_ref):
    core = where_ref[0]
    block = lax.dot_general(
        coefs_ref[...], geno_ref[...], (((1,), (1,)), ((), ())), preferred_element_type=jnp.float32
    )
    out_ref[core] = block[:HALF]
    out_ref[1 - core] = block[HALF:]


def eta_halves(where, genotype, coefs):
    rows, depth = genotype.shape
    block = 256
    return pl.pallas_call(
        eta_kernel,
        grid_spec=pltpu.PrefetchScalarGridSpec(
            num_scalar_prefetch=1,
            grid=(rows // block,),
            in_specs=[
                pl.BlockSpec((block, depth), lambda i, w: (i, 0)),
                pl.BlockSpec((COLS, depth), lambda i, w: (0, 0)),
            ],
            out_specs=pl.BlockSpec((2, HALF, block), lambda i, w: (0, 0, i)),
        ),
        out_shape=jax.ShapeDtypeStruct((2, HALF, rows), jnp.float32),
        compiler_params=pltpu.CompilerParams(vmem_limit_bytes=56 * MIB),
        cost_estimate=pl.CostEstimate(
            flops=2 * rows * depth * 128, bytes_accessed=rows * depth * 2, transcendentals=0
        ),
    )(where, genotype, coefs)


def weight_kernel(where_ref, eta_ref, folds_ref, events_ref, groups_ref, weight_ref, counted_ref, pack_ref):
    core = where_ref[0]
    base = where_ref[1] * (SLOTS - 1)
    fold = folds_ref[pl.ds(pl.multiple_of(core * HALF, 8), HALF), :].astype(jnp.float32)
    weight = fold * jnp.exp(eta_ref[...])
    counted = fold * events_ref[...].astype(jnp.float32)
    weight_ref[...] = weight
    counted_ref[...] = counted
    slot = lax.broadcasted_iota(jnp.int32, (SLOTS, ROWS), 0)
    hot = (slot == groups_ref[...] - base).astype(jnp.bfloat16)

    def total(part):
        return lax.dot_general(
            part, hot, (((1,), (1,)), ((), ())), preferred_element_type=jnp.float32
        )

    high, mid, low = parts3(weight)
    sums = total(high) + (total(mid) + total(low))
    pack = jnp.concatenate([sums, total(counted.astype(jnp.bfloat16))], axis=1).astype(jnp.bfloat16)
    for device in range(COUNT):
        pack_ref[device] = pack


def weights(where, eta, folds, events, groups):
    return pl.pallas_call(
        weight_kernel,
        in_specs=[smem()] + [vmem()] * 4,
        out_specs=[vmem()] * 3,
        out_shape=[
            jax.ShapeDtypeStruct((HALF, ROWS), jnp.float32),
            jax.ShapeDtypeStruct((HALF, ROWS), jnp.float32),
            jax.ShapeDtypeStruct((COUNT, HALF, 2 * SLOTS), jnp.bfloat16),
        ],
        compiler_params=pltpu.CompilerParams(vmem_limit_bytes=16 * MIB),
        cost_estimate=pl.CostEstimate(flops=10**8, bytes_accessed=10**6, transcendentals=0),
    )(where, eta, folds, events, groups)


def resid_kernel(where_ref, pack_ref, weight_ref, counted_ref, groups_ref, resid_ref):
    mine = where_ref[1]
    base = mine * (SLOTS - 1)
    wide = 2 * SLOTS
    source = lax.broadcasted_iota(jnp.int32, (wide, 3 * wide), 0)
    target = lax.broadcasted_iota(jnp.int32, (wide, 3 * wide), 1)
    suffix_part = (target < SLOTS) & (source >= target) & (source < SLOTS)
    total_part = (target >= wide) & (target < 2 * wide) & (source < SLOTS)
    count_part = (target >= 2 * wide) & (source - SLOTS == target - 2 * wide)
    matrix = jnp.where(suffix_part | total_part | count_part, 1.0, 0.0).astype(jnp.bfloat16)
    flat = pack_ref[...].astype(jnp.float32).reshape(COUNT * HALF, wide).astype(jnp.bfloat16)
    sums = jnp.dot(flat, matrix, preferred_element_type=jnp.float32)
    zero = jnp.zeros((HALF, wide), jnp.float32)
    after, before, own = zero, zero, zero
    for device in reversed(range(COUNT)):
        part = sums[device * HALF : device * HALF + HALF]
        count = part[:, 2 * wide :]
        some = count > 0
        risk = jnp.where(some, part[:, :wide] + after, 1.0)
        added = jnp.where(some, count / risk, 0.0)
        after = after + part[:, wide : 2 * wide]
        before = before + jnp.where(device < mine, added, 0.0)
        own = own + jnp.where(device == mine, added, 0.0)
    slot = lax.broadcasted_iota(jnp.int32, (wide, ROWS), 0)
    upto = (slot <= groups_ref[...] - base).astype(jnp.bfloat16)
    high, mid, low = parts3(own)
    hazard = jnp.dot(high, upto, preferred_element_type=jnp.float32) + (
        jnp.dot(mid, upto, preferred_element_type=jnp.float32)
        + jnp.dot(low, upto, preferred_element_type=jnp.float32)
    )
    hazard = hazard + jnp.sum(before, axis=1, keepdims=True)
    resid = counted_ref[...] - weight_ref[...] * hazard
    resid_ref[...] = resid.astype(jnp.bfloat16)


def residuals(where, pack, weight, counted, groups):
    return pl.pallas_call(
        resid_kernel,
        in_specs=[smem()] + [vmem()] * 4,
        out_specs=vmem(),
        out_shape=jax.ShapeDtypeStruct((HALF, ROWS), jnp.bfloat16),
        compiler_params=pltpu.CompilerParams(vmem_limit_bytes=16 * MIB),
        cost_estimate=pl.CostEstimate(flops=10**8, bytes_accessed=10**6, transcendentals=0),
    )(where, pack, weight, counted, groups)


def grad_kernel(where_ref, geno_ref, own_ref, other_ref, out_ref, turned):
    @pl.when(pl.program_id(0) == 0)
    def _():
        first = where_ref[0] == 0
        own = own_ref[...].astype(jnp.float32)
        other = other_ref[...].astype(jnp.float32)
        both = jnp.concatenate(
            [jnp.where(first, own, other), jnp.where(first, other, own)], axis=0
        )
        turned[...] = both.astype(jnp.bfloat16)

    block = jnp.dot(turned[...], geno_ref[...], preferred_element_type=jnp.float32) * SCALE
    for piece in range(geno_ref.shape[1] // 128):
        out_ref[piece] = block[:, 128 * piece : 128 * piece + 128].astype(out_ref.dtype)


def grad_slots(dtype, where, genotype, own, other):
    rows, depth = genotype.shape
    block = 512
    return pl.pallas_call(
        grad_kernel,
        grid_spec=pltpu.PrefetchScalarGridSpec(
            num_scalar_prefetch=1,
            grid=(depth // block,),
            in_specs=[
                pl.BlockSpec((rows, block), lambda i, w: (0, i)),
                pl.BlockSpec((HALF, rows), lambda i, w: (0, 0)),
                pl.BlockSpec((HALF, rows), lambda i, w: (0, 0)),
            ],
            out_specs=pl.BlockSpec((block // 128, COLS, 128), lambda i, w: (i, 0, 0)),
            scratch_shapes=[pltpu.VMEM((COLS, rows), jnp.bfloat16)],
        ),
        out_shape=jax.ShapeDtypeStruct((depth // 128, COLS, 128), dtype),
        compiler_params=pltpu.CompilerParams(vmem_limit_bytes=32 * MIB),
        cost_estimate=pl.CostEstimate(
            flops=2 * rows * depth * 128, bytes_accessed=rows * depth * 2, transcendentals=0
        ),
    )(where, genotype, own, other)


def swap(value, mask):
    return lax.ppermute(value, "var", [(index, index ^ mask) for index in range(8)])


def per_device(genotype, coefs, events, folds, groups):
    subj = lax.axis_index("subj")
    var = lax.axis_index("var")
    where = jnp.stack([var & 1, subj]).astype(jnp.int32)
    events = events.reshape(1, ROWS)
    groups = groups.reshape(1, ROWS)

    eta = eta_halves(where, genotype, coefs.T)
    eta = eta[0] + swap(eta[1], 1)
    sent = eta.astype(jnp.float16)
    for mask in (2, 4, 6):
        eta = eta + swap(sent, mask).astype(jnp.float32)
    weight, counted, pack = weights(where, eta, folds.T, events, groups)
    pack = lax.all_to_all(pack, "subj", 0, 0)
    own = residuals(where, pack, weight, counted, groups)
    other = swap(own, 1)
    slots = grad_slots(jnp.float32, where, genotype, own, other).astype(jnp.float16)
    slots = lax.all_to_all(slots, "subj", 0, 0)
    factor = -1.0 / (SCALE * float(COUNT * ROWS) ** 0.5)
    return (jnp.sum(slots.astype(jnp.float32), axis=0) * factor).T


def solution(mesh):
    in_specs = (P("subj", "var"), P("var", None), P("subj"), P("subj", None), P("subj"))
    out_specs = P(("var", "subj"), None)
    return jax.shard_map(
        per_device, mesh=mesh, in_specs=in_specs, out_specs=out_specs, check_vma=False
    )
```

```python
import jax
import jax.numpy as jnp
from jax import lax
from jax.experimental import pallas as pl
from jax.experimental.pallas import tpu as pltpu
from jax.sharding import PartitionSpec as P

COLS = 48
HALF = 24
ROWS = 1024
SLOTS = 64
COUNT = 32
MIB = 1024 * 1024
SCALE = 0.125


def parts3(value):
    high = value.astype(jnp.bfloat16)
    rest = value - high.astype(jnp.float32)
    mid = rest.astype(jnp.bfloat16)
    low = (rest - mid.astype(jnp.float32)).astype(jnp.bfloat16)
    return high, mid, low


def vmem():
    return pl.BlockSpec(memory_space=pltpu.VMEM)


def hbm():
    return pl.BlockSpec(memory_space=pltpu.HBM)


def blocks(rows, depth):
    return [(row, 512, at, 512) for row in range(0, rows, 512) for at in range(0, depth, 512)]


def eta_kernel(geno_ref, coefs_ref, out_ref, held_ref, taken, sems, taken_sem):
    core = lax.axis_index("var") & 1
    rows, depth = geno_ref.shape
    pieces = blocks(rows, depth)
    take = pltpu.make_async_copy(coefs_ref, taken, taken_sem)
    take.start()
    copies = []
    for number, (row, high, at, wide) in enumerate(pieces):
        window = (pl.ds(row, high), pl.ds(at, wide))
        copy = pltpu.make_async_copy(geno_ref.at[window], held_ref.at[window], sems.at[number])
        copy.start()
        copies.append(copy)
    take.wait()
    total = None
    for number, (row, high, at, wide) in enumerate(pieces):
        copies[number].wait()
        block = lax.dot_general(
            taken[:, at : at + wide],
            held_ref[row : row + high, at : at + wide],
            (((1,), (1,)), ((), ())),
            preferred_element_type=jnp.float32,
        )
        total = block if at == 0 else total + block
        if at + wide == depth:
            out_ref[core, :, row : row + high] = total[:HALF]
            out_ref[1 - core, :, row : row + high] = total[HALF:]


def eta_halves(genotype, coefs):
    rows, depth = genotype.shape
    return pl.pallas_call(
        eta_kernel,
        in_specs=[hbm(), hbm()],
        out_specs=[vmem(), vmem()],
        out_shape=[
            jax.ShapeDtypeStruct((2, HALF, rows), jnp.float32),
            jax.ShapeDtypeStruct((rows, depth), genotype.dtype),
        ],
        scratch_shapes=[
            pltpu.VMEM((COLS, depth), coefs.dtype),
            pltpu.SemaphoreType.DMA((len(blocks(rows, depth)),)),
            pltpu.SemaphoreType.DMA,
        ],
        compiler_params=pltpu.CompilerParams(vmem_limit_bytes=44 * MIB),
        cost_estimate=pl.CostEstimate(
            flops=2 * rows * depth * 128, bytes_accessed=rows * depth * 2, transcendentals=0
        ),
    )(genotype, coefs)


def weight_kernel(eta_ref, folds_ref, events_ref, groups_ref, weight_ref, counted_ref, pack_ref):
    core = lax.axis_index("var") & 1
    base = lax.axis_index("subj") * (SLOTS - 1)
    fold = folds_ref[pl.ds(pl.multiple_of(core * HALF, 8), HALF), :].astype(jnp.float32)
    weight = fold * jnp.exp(eta_ref[...])
    counted = fold * events_ref[...].astype(jnp.float32)
    weight_ref[...] = weight
    counted_ref[...] = counted
    slot = lax.broadcasted_iota(jnp.int32, (SLOTS, ROWS), 0)
    hot = (slot == groups_ref[...] - base).astype(jnp.bfloat16)

    def total(part):
        return lax.dot_general(
            part, hot, (((1,), (1,)), ((), ())), preferred_element_type=jnp.float32
        )

    high, mid, low = parts3(weight)
    sums = total(high) + (total(mid) + total(low))
    pack = jnp.concatenate([sums, total(counted.astype(jnp.bfloat16))], axis=1).astype(jnp.bfloat16)
    for device in range(COUNT):
        pack_ref[device] = pack


def weights(eta, folds, events, groups):
    return pl.pallas_call(
        weight_kernel,
        in_specs=[vmem()] * 4,
        out_specs=[vmem()] * 3,
        out_shape=[
            jax.ShapeDtypeStruct((HALF, ROWS), jnp.float32),
            jax.ShapeDtypeStruct((HALF, ROWS), jnp.float32),
            jax.ShapeDtypeStruct((COUNT, HALF, 2 * SLOTS), jnp.bfloat16),
        ],
        compiler_params=pltpu.CompilerParams(vmem_limit_bytes=16 * MIB),
        cost_estimate=pl.CostEstimate(flops=10**8, bytes_accessed=10**6, transcendentals=0),
    )(eta, folds, events, groups)


def resid_kernel(pack_ref, weight_ref, counted_ref, groups_ref, resid_ref):
    mine = lax.axis_index("subj")
    base = mine * (SLOTS - 1)
    wide = 2 * SLOTS
    source = lax.broadcasted_iota(jnp.int32, (wide, 3 * wide), 0)
    target = lax.broadcasted_iota(jnp.int32, (wide, 3 * wide), 1)
    suffix_part = (target < SLOTS) & (source >= target) & (source < SLOTS)
    total_part = (target >= wide) & (target < 2 * wide) & (source < SLOTS)
    count_part = (target >= 2 * wide) & (source - SLOTS == target - 2 * wide)
    matrix = jnp.where(suffix_part | total_part | count_part, 1.0, 0.0).astype(jnp.bfloat16)
    flat = pack_ref[...].astype(jnp.float32).reshape(COUNT * HALF, wide).astype(jnp.bfloat16)
    sums = jnp.dot(flat, matrix, preferred_element_type=jnp.float32)
    zero = jnp.zeros((HALF, wide), jnp.float32)
    after, before, own = zero, zero, zero
    for device in reversed(range(COUNT)):
        part = sums[device * HALF : device * HALF + HALF]
        count = part[:, 2 * wide :]
        some = count > 0
        risk = jnp.where(some, part[:, :wide] + after, 1.0)
        added = jnp.where(some, count / risk, 0.0)
        after = after + part[:, wide : 2 * wide]
        before = before + jnp.where(device < mine, added, 0.0)
        own = own + jnp.where(device == mine, added, 0.0)
    slot = lax.broadcasted_iota(jnp.int32, (wide, ROWS), 0)
    upto = (slot <= groups_ref[...] - base).astype(jnp.bfloat16)
    high, mid, low = parts3(own)
    hazard = jnp.dot(high, upto, preferred_element_type=jnp.float32) + (
        jnp.dot(mid, upto, preferred_element_type=jnp.float32)
        + jnp.dot(low, upto, preferred_element_type=jnp.float32)
    )
    hazard = hazard + jnp.sum(before, axis=1, keepdims=True)
    resid = counted_ref[...] - weight_ref[...] * hazard
    resid_ref[...] = resid.astype(jnp.bfloat16)


def residuals(pack, weight, counted, groups):
    return pl.pallas_call(
        resid_kernel,
        in_specs=[vmem()] * 4,
        out_specs=vmem(),
        out_shape=jax.ShapeDtypeStruct((HALF, ROWS), jnp.bfloat16),
        compiler_params=pltpu.CompilerParams(vmem_limit_bytes=16 * MIB),
        cost_estimate=pl.CostEstimate(flops=10**8, bytes_accessed=10**6, transcendentals=0),
    )(pack, weight, counted, groups)


def grad_kernel(geno_ref, own_ref, other_ref, out_ref):
    first = (lax.axis_index("var") & 1) == 0
    own = own_ref[...].astype(jnp.float32)
    other = other_ref[...].astype(jnp.float32)
    turned = jnp.concatenate(
        [jnp.where(first, own, other), jnp.where(first, other, own)], axis=0
    ).astype(jnp.bfloat16)
    wide = 2048
    for at in range(0, geno_ref.shape[1], wide):
        block = jnp.dot(turned, geno_ref[:, at : at + wide], preferred_element_type=jnp.float32)
        block = block * SCALE
        for piece in range(wide // 128):
            out_ref[at // 128 + piece] = block[:, 128 * piece : 128 * piece + 128]


def grad_slots(genotype, own, other):
    rows, depth = genotype.shape
    return pl.pallas_call(
        grad_kernel,
        in_specs=[vmem()] * 3,
        out_specs=vmem(),
        out_shape=jax.ShapeDtypeStruct((depth // 128, COLS, 128), jnp.float32),
        compiler_params=pltpu.CompilerParams(vmem_limit_bytes=32 * MIB),
        cost_estimate=pl.CostEstimate(
            flops=2 * rows * depth * 128, bytes_accessed=rows * depth * 2, transcendentals=0
        ),
    )(genotype, own, other)


def swap(value, masks):
    pairs = [(index, index ^ masks[index & 1]) for index in range(8)]
    return lax.ppermute(value, "var", pairs)


def per_device(genotype, coefs, events, folds, groups):
    events = events.reshape(1, ROWS)
    groups = groups.reshape(1, ROWS)

    eta, held = eta_halves(genotype, pltpu.with_memory_space_constraint(coefs.T, pltpu.HBM))
    eta = eta[0] + swap(eta[1], (1, 1))
    sent = eta.astype(jnp.float16)
    for masks in ((2, 6), (6, 2), (4, 4)):
        eta = eta + swap(sent, masks).astype(jnp.float32)
    weight, counted, pack = weights(eta, folds.T, events, groups)
    pack = lax.all_to_all(pack, "subj", 0, 0)
    own = residuals(pack, weight, counted, groups)
    other = swap(own, (1, 1))
    slots = grad_slots(held, own, other).astype(jnp.float16)
    slots = lax.all_to_all(slots, "subj", 0, 0)
    factor = -1.0 / (SCALE * float(COUNT * ROWS) ** 0.5)
    return (jnp.sum(slots.astype(jnp.float32), axis=0) * factor).T


def solution(mesh):
    in_specs = (P("subj", "var"), P("var", None), P("subj"), P("subj", None), P("subj"))
    out_specs = P(("var", "subj"), None)
    return jax.shard_map(
        per_device, mesh=mesh, in_specs=in_specs, out_specs=out_specs, check_vma=False
    )
```

```python
import jax
import jax.numpy as jnp
from jax import lax
from jax.experimental import pallas as pl
from jax.experimental.pallas import tpu as pltpu
from jax.sharding import PartitionSpec as P

COLS = 48
HALF = 24
ROWS = 1024
SLOTS = 64
COUNT = 32
MIB = 1024 * 1024
SCALE = 0.125


def parts3(value):
    high = value.astype(jnp.bfloat16)
    rest = value - high.astype(jnp.float32)
    mid = rest.astype(jnp.bfloat16)
    low = (rest - mid.astype(jnp.float32)).astype(jnp.bfloat16)
    return high, mid, low


def vmem():
    return pl.BlockSpec(memory_space=pltpu.VMEM)


def hbm():
    return pl.BlockSpec(memory_space=pltpu.HBM)


def blocks(depth):
    widths = [256, 256] + [512] * (depth // 512 - 2) + [256, 256]
    return [(sum(widths[:number]), wide) for number, wide in enumerate(widths)]


def eta_kernel(geno_ref, coefs_ref, out_ref, held_ref, taken, geno_sems, coefs_sems):
    core = lax.axis_index("var") & 1
    pieces = blocks(geno_ref.shape[1])
    copies = []
    for number, (at, wide) in enumerate(pieces):
        window = (slice(None), pl.ds(at, wide))
        small = pltpu.make_async_copy(
            coefs_ref.at[window], taken.at[window], coefs_sems.at[number]
        )
        large = pltpu.make_async_copy(
            geno_ref.at[window], held_ref.at[window], geno_sems.at[number]
        )
        small.start()
        large.start()
        copies.append((small, large))
    total = None
    for (at, wide), (small, large) in zip(pieces, copies):
        small.wait()
        large.wait()
        block = lax.dot_general(
            taken[:, at : at + wide],
            held_ref[:, at : at + wide],
            (((1,), (1,)), ((), ())),
            preferred_element_type=jnp.float32,
        )
        total = block if total is None else total + block
    out_ref[core] = total[:HALF]
    out_ref[1 - core] = total[HALF:]


def eta_halves(genotype, coefs):
    rows, depth = genotype.shape
    return pl.pallas_call(
        eta_kernel,
        in_specs=[hbm(), hbm()],
        out_specs=[vmem(), vmem()],
        out_shape=[
            jax.ShapeDtypeStruct((2, HALF, rows), jnp.float32),
            jax.ShapeDtypeStruct((rows, depth), genotype.dtype),
        ],
        scratch_shapes=[
            pltpu.VMEM((COLS, depth), coefs.dtype),
            pltpu.SemaphoreType.DMA((len(blocks(depth)),)),
            pltpu.SemaphoreType.DMA((len(blocks(depth)),)),
        ],
        compiler_params=pltpu.CompilerParams(vmem_limit_bytes=44 * MIB),
        cost_estimate=pl.CostEstimate(
            flops=2 * rows * depth * 128, bytes_accessed=rows * depth * 2, transcendentals=0
        ),
    )(genotype, coefs)


def weight_kernel(eta_ref, folds_ref, events_ref, groups_ref, weight_ref, counted_ref, pack_ref):
    core = lax.axis_index("var") & 1
    base = lax.axis_index("subj") * (SLOTS - 1)
    fold = folds_ref[pl.ds(pl.multiple_of(core * HALF, 8), HALF), :].astype(jnp.float32)
    weight = fold * jnp.exp(eta_ref[...])
    counted = fold * events_ref[...].astype(jnp.float32)
    weight_ref[...] = weight
    counted_ref[...] = counted
    slot = lax.broadcasted_iota(jnp.int32, (SLOTS, ROWS), 0)
    hot = (slot == groups_ref[...] - base).astype(jnp.bfloat16)

    def total(part):
        return lax.dot_general(
            part, hot, (((1,), (1,)), ((), ())), preferred_element_type=jnp.float32
        )

    high, mid, low = parts3(weight)
    sums = total(high) + (total(mid) + total(low))
    pack = jnp.concatenate([sums, total(counted.astype(jnp.bfloat16))], axis=1).astype(jnp.bfloat16)
    for device in range(COUNT):
        pack_ref[device] = pack


def weights(eta, folds, events, groups):
    return pl.pallas_call(
        weight_kernel,
        in_specs=[vmem()] * 4,
        out_specs=[vmem()] * 3,
        out_shape=[
            jax.ShapeDtypeStruct((HALF, ROWS), jnp.float32),
            jax.ShapeDtypeStruct((HALF, ROWS), jnp.float32),
            jax.ShapeDtypeStruct((COUNT, HALF, 2 * SLOTS), jnp.bfloat16),
        ],
        compiler_params=pltpu.CompilerParams(vmem_limit_bytes=16 * MIB),
        cost_estimate=pl.CostEstimate(flops=10**8, bytes_accessed=10**6, transcendentals=0),
    )(eta, folds, events, groups)


def resid_kernel(pack_ref, weight_ref, counted_ref, groups_ref, resid_ref):
    mine = lax.axis_index("subj")
    base = mine * (SLOTS - 1)
    wide = 2 * SLOTS
    source = lax.broadcasted_iota(jnp.int32, (wide, 3 * wide), 0)
    target = lax.broadcasted_iota(jnp.int32, (wide, 3 * wide), 1)
    suffix_part = (target < SLOTS) & (source >= target) & (source < SLOTS)
    total_part = (target >= wide) & (target < 2 * wide) & (source < SLOTS)
    count_part = (target >= 2 * wide) & (source - SLOTS == target - 2 * wide)
    matrix = jnp.where(suffix_part | total_part | count_part, 1.0, 0.0).astype(jnp.bfloat16)
    flat = pack_ref[...].astype(jnp.float32).reshape(COUNT * HALF, wide).astype(jnp.bfloat16)
    sums = jnp.dot(flat, matrix, preferred_element_type=jnp.float32)
    zero = jnp.zeros((HALF, wide), jnp.float32)
    after, before, own = zero, zero, zero
    for device in reversed(range(COUNT)):
        part = sums[device * HALF : device * HALF + HALF]
        count = part[:, 2 * wide :]
        some = count > 0
        risk = jnp.where(some, part[:, :wide] + after, 1.0)
        added = jnp.where(some, count / risk, 0.0)
        after = after + part[:, wide : 2 * wide]
        before = before + jnp.where(device < mine, added, 0.0)
        own = own + jnp.where(device == mine, added, 0.0)
    slot = lax.broadcasted_iota(jnp.int32, (wide, ROWS), 0)
    upto = (slot <= groups_ref[...] - base).astype(jnp.bfloat16)
    high, mid, low = parts3(own)
    hazard = jnp.dot(high, upto, preferred_element_type=jnp.float32) + (
        jnp.dot(mid, upto, preferred_element_type=jnp.float32)
        + jnp.dot(low, upto, preferred_element_type=jnp.float32)
    )
    hazard = hazard + jnp.sum(before, axis=1, keepdims=True)
    resid = counted_ref[...] - weight_ref[...] * hazard
    resid_ref[...] = resid.astype(jnp.bfloat16)


def residuals(pack, weight, counted, groups):
    return pl.pallas_call(
        resid_kernel,
        in_specs=[vmem()] * 4,
        out_specs=vmem(),
        out_shape=jax.ShapeDtypeStruct((HALF, ROWS), jnp.bfloat16),
        compiler_params=pltpu.CompilerParams(vmem_limit_bytes=16 * MIB),
        cost_estimate=pl.CostEstimate(flops=10**8, bytes_accessed=10**6, transcendentals=0),
    )(pack, weight, counted, groups)


def grad_kernel(geno_ref, own_ref, other_ref, out_ref):
    first = (lax.axis_index("var") & 1) == 0
    own = own_ref[...].astype(jnp.float32)
    other = other_ref[...].astype(jnp.float32)
    turned = jnp.concatenate(
        [jnp.where(first, own, other), jnp.where(first, other, own)], axis=0
    ).astype(jnp.bfloat16)
    wide = 2048
    for at in range(0, geno_ref.shape[1], wide):
        block = jnp.dot(turned, geno_ref[:, at : at + wide], preferred_element_type=jnp.float32)
        block = block * SCALE
        for piece in range(wide // 128):
            out_ref[at // 128 + piece] = block[:, 128 * piece : 128 * piece + 128]


def grad_slots(genotype, own, other):
    rows, depth = genotype.shape
    return pl.pallas_call(
        grad_kernel,
        in_specs=[vmem()] * 3,
        out_specs=vmem(),
        out_shape=jax.ShapeDtypeStruct((depth // 128, COLS, 128), jnp.float32),
        compiler_params=pltpu.CompilerParams(vmem_limit_bytes=32 * MIB),
        cost_estimate=pl.CostEstimate(
            flops=2 * rows * depth * 128, bytes_accessed=rows * depth * 2, transcendentals=0
        ),
    )(genotype, own, other)


def swap(value, mask):
    pairs = [(index, index ^ mask) for index in range(8)]
    return lax.ppermute(value, "var", pairs)


def per_device(genotype, coefs, events, folds, groups):
    events = events.reshape(1, ROWS)
    groups = groups.reshape(1, ROWS)

    eta, held = eta_halves(genotype, pltpu.with_memory_space_constraint(coefs.T, pltpu.HBM))
    eta = eta[0] + swap(eta[1], 1)
    sent = eta.astype(jnp.float16)
    for mask in (2, 6, 4):
        eta = eta + swap(sent, mask).astype(jnp.float32)
    weight, counted, pack = weights(eta, folds.T, events, groups)
    pack = lax.all_to_all(pack, "subj", 0, 0)
    own = residuals(pack, weight, counted, groups)
    other = swap(own, 1)
    slots = grad_slots(held, own, other).astype(jnp.float16)
    slots = lax.all_to_all(slots, "subj", 0, 0)
    factor = -1.0 / (SCALE * float(COUNT * ROWS) ** 0.5)
    return (jnp.sum(slots.astype(jnp.float32), axis=0) * factor).T


def solution(mesh):
    in_specs = (P("subj", "var"), P("var", None), P("subj"), P("subj", None), P("subj"))
    out_specs = P(("var", "subj"), None)
    return jax.shard_map(
        per_device, mesh=mesh, in_specs=in_specs, out_specs=out_specs, check_vma=False
    )
```

```python
import jax
import jax.numpy as jnp
from jax import lax
from jax.experimental import pallas as pl
from jax.experimental.pallas import tpu as pltpu
from jax.sharding import PartitionSpec as P

COLS = 48
HALF = 24
ROWS = 1024
SLOTS = 64
COUNT = 32
MIB = 1024 * 1024
SCALE = 0.125


def parts(value):
    high = value.astype(jnp.bfloat16)
    return high, (value - high.astype(jnp.float32)).astype(jnp.bfloat16)


def vmem():
    return pl.BlockSpec(memory_space=pltpu.VMEM)


def hbm():
    return pl.BlockSpec(memory_space=pltpu.HBM)


def blocks(depth):
    widths = [256, 256] + [512] * (depth // 512 - 2) + [256, 256]
    return [(sum(widths[:number]), wide) for number, wide in enumerate(widths)]


def eta_kernel(geno_ref, coefs_ref, out_ref, held_ref, taken, geno_sems, coefs_sems):
    core = lax.axis_index("var") & 1
    pieces = blocks(geno_ref.shape[1])
    copies = []
    for number, (at, wide) in enumerate(pieces):
        window = (slice(None), pl.ds(at, wide))
        small = pltpu.make_async_copy(
            coefs_ref.at[window], taken.at[window], coefs_sems.at[number]
        )
        large = pltpu.make_async_copy(
            geno_ref.at[window], held_ref.at[window], geno_sems.at[number]
        )
        small.start()
        large.start()
        copies.append((small, large))
    total = None
    for (at, wide), (small, large) in zip(pieces, copies):
        small.wait()
        large.wait()
        block = lax.dot_general(
            taken[:, at : at + wide],
            held_ref[:, at : at + wide],
            (((1,), (1,)), ((), ())),
            preferred_element_type=jnp.float32,
        )
        total = block if total is None else total + block
    out_ref[core] = total[:HALF]
    out_ref[1 - core] = total[HALF:]


def eta_halves(genotype, coefs):
    rows, depth = genotype.shape
    return pl.pallas_call(
        eta_kernel,
        in_specs=[hbm(), hbm()],
        out_specs=[vmem(), vmem()],
        out_shape=[
            jax.ShapeDtypeStruct((2, HALF, rows), jnp.float32),
            jax.ShapeDtypeStruct((rows, depth), genotype.dtype),
        ],
        scratch_shapes=[
            pltpu.VMEM((COLS, depth), coefs.dtype),
            pltpu.SemaphoreType.DMA((len(blocks(depth)),)),
            pltpu.SemaphoreType.DMA((len(blocks(depth)),)),
        ],
        compiler_params=pltpu.CompilerParams(vmem_limit_bytes=44 * MIB),
        cost_estimate=pl.CostEstimate(
            flops=2 * rows * depth * 128, bytes_accessed=rows * depth * 2, transcendentals=0
        ),
    )(genotype, coefs)


def rows_dot(left, right):
    return lax.dot_general(
        left, right, (((1,), (1,)), ((), ())), preferred_element_type=jnp.float32
    )


def plan_kernel(folds_ref, events_ref, groups_ref, fold_ref, counted_ref, hot_ref, upto_ref, count_ref, scan_ref):
    core = lax.axis_index("var") & 1
    base = lax.axis_index("subj") * (SLOTS - 1)
    fold = folds_ref[pl.ds(pl.multiple_of(core * HALF, 8), HALF), :].astype(jnp.float32)
    counted = fold * events_ref[...].astype(jnp.float32)
    fold_ref[...] = fold
    counted_ref[...] = counted
    slot = lax.broadcasted_iota(jnp.int32, (SLOTS, ROWS), 0)
    group = groups_ref[...] - base
    hot = (slot == group).astype(jnp.bfloat16)
    hot_ref[...] = hot
    upto_ref[...] = (slot <= group).astype(jnp.bfloat16)
    count_ref[...] = rows_dot(counted.astype(jnp.bfloat16), hot)
    wide = 2 * SLOTS
    source = lax.broadcasted_iota(jnp.int32, (wide, 2 * wide), 0)
    target = lax.broadcasted_iota(jnp.int32, (wide, 2 * wide), 1)
    suffix_part = (target < SLOTS) & (source >= target) & (source < SLOTS)
    total_part = (target >= wide) & (source < SLOTS)
    scan_ref[...] = jnp.where(suffix_part | total_part, 1.0, 0.0).astype(jnp.bfloat16)


def plan(folds, events, groups):
    return pl.pallas_call(
        plan_kernel,
        in_specs=[vmem()] * 3,
        out_specs=[vmem()] * 6,
        out_shape=[
            jax.ShapeDtypeStruct((HALF, ROWS), jnp.float32),
            jax.ShapeDtypeStruct((HALF, ROWS), jnp.float32),
            jax.ShapeDtypeStruct((SLOTS, ROWS), jnp.bfloat16),
            jax.ShapeDtypeStruct((SLOTS, ROWS), jnp.bfloat16),
            jax.ShapeDtypeStruct((HALF, SLOTS), jnp.float32),
            jax.ShapeDtypeStruct((2 * SLOTS, 4 * SLOTS), jnp.bfloat16),
        ],
        compiler_params=pltpu.CompilerParams(vmem_limit_bytes=16 * MIB),
        cost_estimate=pl.CostEstimate(flops=10**8, bytes_accessed=10**6, transcendentals=0),
    )(folds, events, groups)


def weight_kernel(eta_ref, fold_ref, hot_ref, count_ref, weight_ref, pack_ref):
    weight = fold_ref[...] * jnp.exp(eta_ref[...])
    weight_ref[...] = weight
    high, low = parts(weight)
    sums = rows_dot(high, hot_ref[...]) + rows_dot(low, hot_ref[...])
    pack = jnp.concatenate([sums, count_ref[...]], axis=1).astype(jnp.bfloat16)
    for device in range(COUNT):
        pack_ref[device] = pack


def weights(eta, fold, hot, count):
    return pl.pallas_call(
        weight_kernel,
        in_specs=[vmem()] * 4,
        out_specs=[vmem()] * 2,
        out_shape=[
            jax.ShapeDtypeStruct((HALF, ROWS), jnp.float32),
            jax.ShapeDtypeStruct((COUNT, HALF, 2 * SLOTS), jnp.bfloat16),
        ],
        compiler_params=pltpu.CompilerParams(vmem_limit_bytes=16 * MIB),
        cost_estimate=pl.CostEstimate(flops=10**8, bytes_accessed=10**6, transcendentals=0),
    )(eta, fold, hot, count)


def resid_kernel(pack_ref, weight_ref, counted_ref, upto_ref, scan_ref, resid_ref):
    mine = lax.axis_index("subj")
    wide = 2 * SLOTS
    flat = pack_ref[...].astype(jnp.float32).reshape(COUNT * HALF, wide)
    sums = jnp.dot(flat.astype(jnp.bfloat16), scan_ref[...], preferred_element_type=jnp.float32)
    counts = pltpu.roll(flat, SLOTS, 1)
    zero = jnp.zeros((HALF, wide), jnp.float32)
    after, before, own = zero, zero, zero
    for device in reversed(range(COUNT)):
        part = sums[device * HALF : device * HALF + HALF]
        count = counts[device * HALF : device * HALF + HALF]
        some = count > 0
        risk = jnp.where(some, part[:, :wide] + after, 1.0)
        added = jnp.where(some, count / risk, 0.0)
        after = after + part[:, wide:]
        before = before + jnp.where(device < mine, added, 0.0)
        own = own + jnp.where(device == mine, added, 0.0)
    before = jnp.where(lax.broadcasted_iota(jnp.int32, (HALF, wide), 1) < SLOTS, before, 0.0)
    high, low = parts(own[:, :SLOTS])
    hazard = jnp.dot(high, upto_ref[...], preferred_element_type=jnp.float32) + jnp.dot(
        low, upto_ref[...], preferred_element_type=jnp.float32
    )
    hazard = hazard + jnp.sum(before, axis=1, keepdims=True)
    resid = counted_ref[...] - weight_ref[...] * hazard
    resid_ref[...] = resid.astype(jnp.bfloat16)


def residuals(pack, weight, counted, upto, scan):
    return pl.pallas_call(
        resid_kernel,
        in_specs=[vmem()] * 5,
        out_specs=vmem(),
        out_shape=jax.ShapeDtypeStruct((HALF, ROWS), jnp.bfloat16),
        compiler_params=pltpu.CompilerParams(vmem_limit_bytes=16 * MIB),
        cost_estimate=pl.CostEstimate(flops=10**8, bytes_accessed=10**6, transcendentals=0),
    )(pack, weight, counted, upto, scan)


def grad_kernel(geno_ref, own_ref, other_ref, out_ref):
    first = (lax.axis_index("var") & 1) == 0
    own = own_ref[...].astype(jnp.float32)
    other = other_ref[...].astype(jnp.float32)
    turned = jnp.concatenate(
        [jnp.where(first, own, other), jnp.where(first, other, own)], axis=0
    ).astype(jnp.bfloat16)
    wide = 2048
    for at in range(0, geno_ref.shape[1], wide):
        block = jnp.dot(turned, geno_ref[:, at : at + wide], preferred_element_type=jnp.float32)
        block = block * SCALE
        for piece in range(wide // 128):
            out_ref[at // 128 + piece] = block[:, 128 * piece : 128 * piece + 128]


def grad_slots(genotype, own, other):
    rows, depth = genotype.shape
    return pl.pallas_call(
        grad_kernel,
        in_specs=[vmem()] * 3,
        out_specs=vmem(),
        out_shape=jax.ShapeDtypeStruct((depth // 128, COLS, 128), jnp.float32),
        compiler_params=pltpu.CompilerParams(vmem_limit_bytes=32 * MIB),
        cost_estimate=pl.CostEstimate(
            flops=2 * rows * depth * 128, bytes_accessed=rows * depth * 2, transcendentals=0
        ),
    )(genotype, own, other)


def swap(value, mask):
    pairs = [(index, index ^ mask) for index in range(8)]
    return lax.ppermute(value, "var", pairs)


def per_device(genotype, coefs, events, folds, groups):
    events = events.reshape(1, ROWS)
    groups = groups.reshape(1, ROWS)

    eta, held = eta_halves(genotype, pltpu.with_memory_space_constraint(coefs.T, pltpu.HBM))
    fold, counted, hot, upto, count, scan = plan(folds.T, events, groups)
    eta = eta[0] + swap(eta[1], 1)
    sent = eta.astype(jnp.float16)
    for mask in (2, 6, 4):
        eta = eta + swap(sent, mask).astype(jnp.float32)
    weight, pack = weights(eta, fold, hot, count)
    pack = lax.all_to_all(pack, "subj", 0, 0)
    own = residuals(pack, weight, counted, upto, scan)
    other = swap(own, 1)
    slots = grad_slots(held, own, other).astype(jnp.float16)
    slots = lax.all_to_all(slots, "subj", 0, 0)
    factor = -1.0 / (SCALE * float(COUNT * ROWS) ** 0.5)
    return (jnp.sum(slots.astype(jnp.float32), axis=0) * factor).T


def solution(mesh):
    in_specs = (P("subj", "var"), P("var", None), P("subj"), P("subj", None), P("subj"))
    out_specs = P(("var", "subj"), None)
    return jax.shard_map(
        per_device, mesh=mesh, in_specs=in_specs, out_specs=out_specs, check_vma=False
    )
```

```python
import jax
import jax.numpy as jnp
from jax import lax
from jax.experimental import pallas as pl
from jax.experimental.pallas import tpu as pltpu
from jax.sharding import PartitionSpec as P

COLS = 48
HALF = 24
ROWS = 1024
SLOTS = 64
COUNT = 32
MIB = 1024 * 1024
SCALE = 0.125


def parts(value):
    high = value.astype(jnp.bfloat16)
    return high, (value - high.astype(jnp.float32)).astype(jnp.bfloat16)


def vmem():
    return pl.BlockSpec(memory_space=pltpu.VMEM)


def hbm():
    return pl.BlockSpec(memory_space=pltpu.HBM)


def blocks(depth):
    widths = [256, 256] + [512] * (depth // 512 - 2) + [256, 256]
    return [(sum(widths[:number]), wide) for number, wide in enumerate(widths)]


def eta_kernel(geno_ref, coefs_ref, out_ref, held_ref, taken, geno_sems, coefs_sems):
    core = lax.axis_index("var") & 1
    pieces = blocks(geno_ref.shape[1])
    copies = []
    for number, (at, wide) in enumerate(pieces):
        window = (slice(None), pl.ds(at, wide))
        small = pltpu.make_async_copy(
            coefs_ref.at[window], taken.at[window], coefs_sems.at[number]
        )
        large = pltpu.make_async_copy(
            geno_ref.at[window], held_ref.at[window], geno_sems.at[number]
        )
        small.start()
        large.start()
        copies.append((small, large))
    total = None
    for (at, wide), (small, large) in zip(pieces, copies):
        small.wait()
        large.wait()
        block = lax.dot_general(
            taken[:, at : at + wide],
            held_ref[:, at : at + wide],
            (((1,), (1,)), ((), ())),
            preferred_element_type=jnp.float32,
        )
        total = block if total is None else total + block
    out_ref[core] = total[:HALF]
    out_ref[1 - core] = total[HALF:]


def eta_halves(genotype, coefs):
    rows, depth = genotype.shape
    return pl.pallas_call(
        eta_kernel,
        in_specs=[hbm(), hbm()],
        out_specs=[vmem(), vmem()],
        out_shape=[
            jax.ShapeDtypeStruct((2, HALF, rows), jnp.float32),
            jax.ShapeDtypeStruct((rows, depth), genotype.dtype),
        ],
        scratch_shapes=[
            pltpu.VMEM((COLS, depth), coefs.dtype),
            pltpu.SemaphoreType.DMA((len(blocks(depth)),)),
            pltpu.SemaphoreType.DMA((len(blocks(depth)),)),
        ],
        compiler_params=pltpu.CompilerParams(vmem_limit_bytes=44 * MIB),
        cost_estimate=pl.CostEstimate(
            flops=2 * rows * depth * 128, bytes_accessed=rows * depth * 2, transcendentals=0
        ),
    )(genotype, coefs)


def rows_dot(left, right):
    return lax.dot_general(
        left, right, (((1,), (1,)), ((), ())), preferred_element_type=jnp.float32
    )


def plan_kernel(folds_ref, events_ref, groups_ref, fold_ref, counted_ref, hot_ref, upto_ref, count_ref, scan_ref):
    core = lax.axis_index("var") & 1
    base = lax.axis_index("subj") * (SLOTS - 1)
    fold = folds_ref[pl.ds(pl.multiple_of(core * HALF, 8), HALF), :].astype(jnp.float32)
    counted = fold * events_ref[...].astype(jnp.float32)
    fold_ref[...] = fold
    counted_ref[...] = counted
    slot = lax.broadcasted_iota(jnp.int32, (SLOTS, ROWS), 0)
    group = groups_ref[...] - base
    hot = (slot == group).astype(jnp.bfloat16)
    hot_ref[...] = hot
    upto_ref[...] = (slot <= group).astype(jnp.bfloat16)
    count_ref[...] = rows_dot(counted.astype(jnp.bfloat16), hot)
    wide = 2 * SLOTS
    source = lax.broadcasted_iota(jnp.int32, (wide, 2 * wide), 0)
    target = lax.broadcasted_iota(jnp.int32, (wide, 2 * wide), 1)
    suffix_part = (target < SLOTS) & (source >= target) & (source < SLOTS)
    total_part = (target >= wide) & (source < SLOTS)
    scan_ref[...] = jnp.where(suffix_part | total_part, 1.0, 0.0).astype(jnp.bfloat16)


def plan(folds, events, groups):
    return pl.pallas_call(
        plan_kernel,
        in_specs=[vmem()] * 3,
        out_specs=[vmem()] * 6,
        out_shape=[
            jax.ShapeDtypeStruct((HALF, ROWS), jnp.float32),
            jax.ShapeDtypeStruct((HALF, ROWS), jnp.float32),
            jax.ShapeDtypeStruct((SLOTS, ROWS), jnp.bfloat16),
            jax.ShapeDtypeStruct((SLOTS, ROWS), jnp.bfloat16),
            jax.ShapeDtypeStruct((HALF, SLOTS), jnp.float32),
            jax.ShapeDtypeStruct((2 * SLOTS, 4 * SLOTS), jnp.bfloat16),
        ],
        compiler_params=pltpu.CompilerParams(vmem_limit_bytes=16 * MIB),
        cost_estimate=pl.CostEstimate(flops=10**8, bytes_accessed=10**6, transcendentals=0),
    )(folds, events, groups)


def weight_kernel(eta_ref, fold_ref, hot_ref, count_ref, weight_ref, pack_ref):
    weight = fold_ref[...] * jnp.exp(eta_ref[...])
    weight_ref[...] = weight
    high, low = parts(weight)
    sums = rows_dot(high, hot_ref[...]) + rows_dot(low, hot_ref[...])
    pack = jnp.concatenate([sums, count_ref[...]], axis=1).astype(jnp.bfloat16)
    for device in range(COUNT):
        pack_ref[device] = pack


def weights(eta, fold, hot, count):
    return pl.pallas_call(
        weight_kernel,
        in_specs=[vmem()] * 4,
        out_specs=[vmem()] * 2,
        out_shape=[
            jax.ShapeDtypeStruct((HALF, ROWS), jnp.float32),
            jax.ShapeDtypeStruct((COUNT, HALF, 2 * SLOTS), jnp.bfloat16),
        ],
        compiler_params=pltpu.CompilerParams(vmem_limit_bytes=16 * MIB),
        cost_estimate=pl.CostEstimate(flops=10**8, bytes_accessed=10**6, transcendentals=0),
    )(eta, fold, hot, count)


def resid_kernel(pack_ref, weight_ref, counted_ref, upto_ref, scan_ref, resid_ref):
    mine = lax.axis_index("subj")
    wide = 2 * SLOTS
    flat = pack_ref[...].astype(jnp.float32).reshape(COUNT * HALF, wide)
    sums = jnp.dot(flat.astype(jnp.bfloat16), scan_ref[...], preferred_element_type=jnp.float32)
    counts = pltpu.roll(flat, SLOTS, 1)
    zero = jnp.zeros((HALF, wide), jnp.float32)
    after, before, own = zero, zero, zero
    for device in reversed(range(COUNT)):
        part = sums[device * HALF : device * HALF + HALF]
        count = counts[device * HALF : device * HALF + HALF]
        some = count > 0
        risk = jnp.where(some, part[:, :wide] + after, 1.0)
        added = jnp.where(some, count / risk, 0.0)
        after = after + part[:, wide:]
        before = before + jnp.where(device < mine, added, 0.0)
        own = own + jnp.where(device == mine, added, 0.0)
    before = jnp.where(lax.broadcasted_iota(jnp.int32, (HALF, wide), 1) < SLOTS, before, 0.0)
    high, low = parts(own[:, :SLOTS])
    hazard = jnp.dot(high, upto_ref[...], preferred_element_type=jnp.float32) + jnp.dot(
        low, upto_ref[...], preferred_element_type=jnp.float32
    )
    hazard = hazard + jnp.sum(before, axis=1, keepdims=True)
    resid = counted_ref[...] - weight_ref[...] * hazard
    resid_ref[...] = resid.astype(jnp.bfloat16)


def residuals(pack, weight, counted, upto, scan):
    return pl.pallas_call(
        resid_kernel,
        in_specs=[vmem()] * 5,
        out_specs=vmem(),
        out_shape=jax.ShapeDtypeStruct((HALF, ROWS), jnp.bfloat16),
        compiler_params=pltpu.CompilerParams(vmem_limit_bytes=16 * MIB),
        cost_estimate=pl.CostEstimate(flops=10**8, bytes_accessed=10**6, transcendentals=0),
    )(pack, weight, counted, upto, scan)


def grad_kernel(geno_ref, own_ref, other_ref, out_ref):
    first = (lax.axis_index("var") & 1) == 0
    own = own_ref[...].astype(jnp.float32)
    other = other_ref[...].astype(jnp.float32)
    turned = jnp.concatenate(
        [jnp.where(first, own, other), jnp.where(first, other, own)], axis=0
    ).astype(jnp.bfloat16)
    wide = 2048
    for at in range(0, geno_ref.shape[1], wide):
        block = jnp.dot(turned, geno_ref[:, at : at + wide], preferred_element_type=jnp.float32)
        block = block * SCALE
        for piece in range(wide // 128):
            out_ref[at // 128 + piece] = block[:, 128 * piece : 128 * piece + 128]


def grad_slots(genotype, own, other):
    rows, depth = genotype.shape
    return pl.pallas_call(
        grad_kernel,
        in_specs=[vmem()] * 3,
        out_specs=vmem(),
        out_shape=jax.ShapeDtypeStruct((depth // 128, COLS, 128), jnp.float32),
        compiler_params=pltpu.CompilerParams(vmem_limit_bytes=32 * MIB),
        cost_estimate=pl.CostEstimate(
            flops=2 * rows * depth * 128, bytes_accessed=rows * depth * 2, transcendentals=0
        ),
    )(genotype, own, other)


def swap(value, mask):
    pairs = [(index, index ^ mask) for index in range(8)]
    return lax.ppermute(value, "var", pairs)


def per_device(genotype, coefs, events, folds, groups):
    events = events.reshape(1, ROWS)
    groups = groups.reshape(1, ROWS)

    eta, held = eta_halves(genotype, pltpu.with_memory_space_constraint(coefs.T, pltpu.HBM))
    fold, counted, hot, upto, count, scan = plan(folds.T, events, groups)
    eta = eta[0] + swap(eta[1], 1)
    sent = eta.astype(jnp.float16)
    for mask in (2, 6, 4):
        eta = eta + swap(sent, mask).astype(jnp.float32)
    weight, pack = weights(eta, fold, hot, count)
    pack = lax.all_to_all(pack, "subj", 0, 0)
    own = residuals(pack, weight, counted, upto, scan)
    other = swap(own, 1)
    slots = grad_slots(held, own, other).astype(jnp.float16)
    slots = lax.all_to_all(slots, "subj", 0, 0)
    factor = -1.0 / (SCALE * float(COUNT * ROWS) ** 0.5)
    return jnp.sum(slots.astype(jnp.float32) * factor, axis=0).T


def solution(mesh):
    in_specs = (P("subj", "var"), P("var", None), P("subj"), P("subj", None), P("subj"))
    out_specs = P(("var", "subj"), None)
    return jax.shard_map(
        per_device, mesh=mesh, in_specs=in_specs, out_specs=out_specs, check_vma=False
    )
```
